32 devices in a mesh: ctx: 2 (over x), exp: 16 (over z, y, core).
Axes of the slice: x: 2, y: 2, z: 4, core: 2. Of those that a mesh axis runs over, the one named last changes fastest.
Arguments:
- queries: bfloat16 [4096, 3072], P('ctx', 'exp'), may hold values from -16 to 16, as said below
- latent: bfloat16 [4096, 576], P('ctx'), may hold values from -6 to 6, as said below
- key_up_weight: bfloat16 [16, 128, 512], P('exp'), may hold values from -0.5 to 0.5
- value_up_weight: bfloat16 [16, 512, 128], P('exp'), may hold values from -1 to 1
- block_order: int32 [16], replicated, may hold values from 0 to 15, each once
- expert_ids: int32 [4096, 8], P(('ctx', 'exp')), may hold values from 0 to 95, as said below
- gates: float32 [4096, 8], P(('ctx', 'exp')), may hold values from 0.05 to 1
- expert_rows: bfloat16 [2, 16, 2, 16, 36, 7168], P('ctx', 'exp'), may hold values from -6 to 6
Outputs:
- attended: bfloat16 [4096, 2048], P('ctx', 'exp')
- combined: bfloat16 [4096, 7168], P(('ctx', 'exp'))
The draws below stay inside these ranges and needn't reach their ends.
Inputs may be any that keep to these rules, and one draw needn't show every extreme that they name: `queries`: queries with their rotary parts already applied. Normed latent and rotary key, rotary parts already applied. `expert_ids`: each row names 8 different experts; expert e belongs to device e // 3. Among the rows of one device's 128 tokens at most 36 pairs name experts of one owning device, and some owning device receives exactly 36 from every device. `block_order`: each of the 16 sequence blocks appears once.
All inputs are finite; a program needn't handle non-finite values.
Results may differ from the reference program's by a relative error of at most 0.0084.
Values may be sent and summed in bfloat16 or wider, within the bound.
No kernel may reach another device: no remote copies, remote signals or barrier semaphores. Data moves between devices by JAX's collectives and lax.ppermute only.
A program may use at most 256 MiB of HBM per device.

```python
import math
import jax
import jax.numpy as jnp
from jax import lax

D = 7168
LATENT_WIDTH = 512
PLAIN_HEAD_WIDTH = 128
ROTARY_WIDTH = 64
VALUE_WIDTH = 128
TOPK = 8
EXP_DEV = 3
SEQ_BLOCKS = 16
TOK_A = 128
PROMPT_LENGTH = 4096
HEAD_TOTAL = 16
TOKENS_A = 4096
CAP = 36
N_CTX = 2
N_EXP = 16


def draw_queries(key, part):
    key = jax.random.fold_in(key, 21)
    head_width = PLAIN_HEAD_WIDTH + ROTARY_WIDTH
    value_rows = jnp.clip(jax.random.normal(key, (PROMPT_LENGTH, HEAD_TOTAL, head_width), jnp.float32), -6.0, 6.0)
    return value_rows.reshape(PROMPT_LENGTH, HEAD_TOTAL * head_width).astype(jnp.bfloat16)


def draw_latent(key, part):
    key = jax.random.fold_in(key, 33)
    value_rows = jnp.clip(jax.random.normal(key, (PROMPT_LENGTH, LATENT_WIDTH + ROTARY_WIDTH), jnp.float32), -6.0, 6.0)
    return value_rows.astype(jnp.bfloat16)


def draw_expert_ids(key, part):
    key = jax.random.fold_in(key, 11)
    devices = N_CTX * N_EXP
    families = devices // TOPK
    remaining = TOK_A - CAP
    single_key, key_two, key_three = jax.random.split(key, 3)
    hot_family = jax.random.randint(single_key, (), 0, families)
    owner_perm = jax.random.permutation(key_two, devices)

    def one_block(block_key):
        key_a, key_b, key_c = jax.random.split(block_key, 3)
        others = jax.random.permutation(key_a, families - 1)
        others = others + (others >= hot_family).astype(others.dtype)
        spread = others[jnp.arange(remaining) * (families - 1) // remaining]
        family_seq = jnp.concatenate([jnp.full((CAP,), hot_family, jnp.int32), spread.astype(jnp.int32)])
        family_seq = jax.random.permutation(key_b, family_seq)
        owners = owner_perm[family_seq[:, None] + families * jnp.arange(TOPK)[None, :]]
        local_expert = jax.random.randint(key_c, (TOK_A, TOPK), 0, EXP_DEV)
        return (owners * EXP_DEV + local_expert).astype(jnp.int32)
    result = jax.vmap(one_block)(jax.random.split(key_three, devices))
    return result.reshape(devices * TOK_A, TOPK).astype(jnp.int32)


def shard_levels(own_key, extent, shards, low, largest):
    loudness, own = 1.0, jax.random.fold_in(own_key, 6)
    for position, parts in shards:
        steps = jnp.exp(jax.random.uniform(jax.random.fold_in(own, position), (parts,), jnp.float32, low / len(shards), largest / len(shards)))
        loudness = loudness * jnp.repeat(steps, extent[position] // parts).reshape([-1 if axis == position else 1 for axis in range(len(extent))])
    return loudness


def bell_draw(rng, shape, width, bound, shards=(), kind=jnp.bfloat16):
    gain = shard_levels(rng, shape, shards, -0.22, 0.18) if shards else 1.0
    values = jax.random.normal(rng, shape, jnp.float32) * width * gain
    return jnp.minimum(jnp.maximum(values, -bound), bound).astype(kind)


def setup_inputs(seed: int = 0) -> dict:
    streams_of = jax.random.split(jax.random.key(seed), 9)
    queries = draw_queries(jax.random.fold_in(streams_of[8], 71), 0)
    latent = draw_latent(jax.random.fold_in(streams_of[8], 71), 0)
    key_up_weight = bell_draw(streams_of[2], (HEAD_TOTAL, PLAIN_HEAD_WIDTH, LATENT_WIDTH), PLAIN_HEAD_WIDTH ** -0.5, 0.5, ((0, 16),))
    value_up_weight = bell_draw(streams_of[3], (HEAD_TOTAL, LATENT_WIDTH, VALUE_WIDTH), (LATENT_WIDTH // 16) ** -0.5, 1.0, ((0, 16),))
    block_order = jax.random.permutation(streams_of[4], SEQ_BLOCKS).astype(jnp.int32)
    expert_ids = draw_expert_ids(jax.random.fold_in(streams_of[8], 71), 0)
    gates = jnp.clip(jnp.exp(math.log(1.0) - 2.9957323 * jax.random.uniform(streams_of[6], (TOKENS_A, TOPK), jnp.float32) ** shard_levels(streams_of[6], (TOKENS_A, TOPK), ((0, 32),), -0.2, 0.2)), 0.05, 1.0)
    expert_rows = bell_draw(streams_of[7], (N_CTX, N_EXP, N_CTX, N_EXP, CAP, D), 1.0, 6.0, ((0, 2), (1, 16)))
    return {"queries": queries, "latent": latent, "key_up_weight": key_up_weight, "value_up_weight": value_up_weight, "block_order": block_order, "expert_ids": expert_ids, "gates": gates, "expert_rows": expert_rows}


ROUTE_SCALE = 2.827

def storage_positions(block_order, seq_len, block_len):
    row_ids = jnp.arange(seq_len, dtype=jnp.int32)
    return (block_order[row_ids // block_len] * block_len + row_ids % block_len).astype(jnp.int32)

def slot_numbers(owners, devices):
    flat_owners = owners.reshape(-1)
    onehot = (flat_owners[:, None] == jnp.arange(devices, dtype=jnp.int32)[None, :]).astype(jnp.int32)
    before = jnp.cumsum(onehot, axis=0) - onehot
    return lax.optimization_barrier(jnp.sum(before * onehot, axis=1)).reshape(owners.shape).astype(jnp.int32)

def reference(queries, latent, key_up_weight, value_up_weight, block_order, expert_ids, gates, expert_rows):
    block_len = PROMPT_LENGTH // SEQ_BLOCKS
    positions = storage_positions(block_order, PROMPT_LENGTH, block_len)
    allowed = positions[None, :] <= positions[:, None]
    per_head = queries.reshape(PROMPT_LENGTH, HEAD_TOTAL, PLAIN_HEAD_WIDTH + ROTARY_WIDTH)
    score_scale = 1.0 / math.sqrt(PLAIN_HEAD_WIDTH + ROTARY_WIDTH)

    def one_head(h):
        query_head = lax.dynamic_index_in_dim(per_head, h, 1, keepdims=False)
        absorb = lax.dynamic_index_in_dim(key_up_weight, h, 0, keepdims=False)
        q_latent = jnp.dot(query_head[:, :PLAIN_HEAD_WIDTH], absorb, preferred_element_type=jnp.float32).astype(jnp.bfloat16)
        query_full = jnp.concatenate([q_latent, query_head[:, PLAIN_HEAD_WIDTH:]], axis=1)
        scores = jnp.dot(query_full, latent.T, preferred_element_type=jnp.float32) * score_scale
        masked = jnp.where(allowed, scores, -1e+30)
        row_max = lax.optimization_barrier(jnp.max(masked, axis=1, keepdims=True))
        attention_probabilities = jnp.where(allowed, jnp.exp(masked - row_max), 0.0)
        weight_sum = lax.optimization_barrier(jnp.sum(attention_probabilities, axis=1, keepdims=True))
        blended_output = jnp.dot(attention_probabilities.astype(jnp.bfloat16), latent[:, :LATENT_WIDTH], preferred_element_type=jnp.float32)
        latent_out = (blended_output / weight_sum).astype(jnp.bfloat16)
        up_weight = lax.dynamic_index_in_dim(value_up_weight, h, 0, keepdims=False)
        return jnp.dot(latent_out, up_weight, preferred_element_type=jnp.float32).astype(jnp.bfloat16)
    heads_out = lax.map(one_head, jnp.arange(HEAD_TOTAL, dtype=jnp.int32))
    attended = jnp.transpose(heads_out, (1, 0, 2)).reshape(PROMPT_LENGTH, HEAD_TOTAL * VALUE_WIDTH)
    devices = N_CTX * N_EXP
    flat_rows = expert_rows.reshape(devices, devices, CAP, D)
    owners = (expert_ids // EXP_DEV).astype(jnp.int32)

    def one_block(b):
        owner_block = lax.dynamic_slice_in_dim(owners, b * TOK_A, TOK_A, 0)
        gate_block = lax.dynamic_slice_in_dim(gates, b * TOK_A, TOK_A, 0)
        slots = slot_numbers(owner_block, devices)
        scaled_gates = ROUTE_SCALE * gate_block / lax.optimization_barrier(jnp.sum(gate_block, axis=1, keepdims=True))
        source = lax.dynamic_index_in_dim(flat_rows, b, 1, keepdims=False).reshape(devices * CAP, D)
        running = jnp.zeros((TOK_A, D), jnp.float32)
        for k in range(TOPK):
            picked = source[owner_block[:, k] * CAP + slots[:, k]]
            running = running + scaled_gates[:, k:k + 1] * picked.astype(jnp.float32)
        return running.astype(jnp.bfloat16)
    combined = lax.map(one_block, jnp.arange(devices, dtype=jnp.int32)).reshape(devices * TOK_A, D)
    return (attended, combined)
```

```python
import functools
import math

import jax
import jax.numpy as jnp
from jax import lax
from jax.experimental import pallas as pl
from jax.experimental.pallas import tpu as pltpu
from jax.sharding import PartitionSpec as P

LATENT_WIDTH = 512
PLAIN_HEAD_WIDTH = 128
ROTARY_WIDTH = 64
VALUE_WIDTH = 128
EXP_DEV = 3
ROUTE_SCALE = 2.827
AXES = ("ctx", "exp")
VMEM_LIMIT = 48 * 1024 * 1024

CHUNKS = (
    (512, "x"),
    (512, "y"),
    (1024, "x"),
    (1024, "y"),
    (1024, "x"),
    (1024, "y"),
    (1024, "x"),
    (1024, "y"),
)


def exchange(value, mask, devices):
    return lax.ppermute(value, AXES, [(i, i ^ mask) for i in range(devices)])


def low_mask(index, masks):
    total = 0
    for place, mask in enumerate(reversed(masks)):
        if (index >> place) & 1:
            total ^= mask
    return total


def pack_kernel(count, me_ref, *refs):
    ins, outs = refs[: 4 * count], refs[4 * count :]
    for quarter in range(4):
        blocks = [ins[quarter * count + d][0] for d in range(count)]
        outs[quarter][...] = jnp.concatenate(blocks, axis=0)


def pack(me, rows, start, width, first, rest):
    devices, capacity, _ = rows.shape
    count = devices // 8
    tile = 512 if width % 512 == 0 and start % 512 == 0 else 256

    def place(quarter, d, g, j, me_ref):
        fixed = (quarter & 1) ^ (first if quarter & 2 else 0) ^ low_mask(d, rest[1:])
        return (me_ref[0] ^ fixed ^ (g * rest[0]), 0, start // tile + j)

    in_specs = [
        pl.BlockSpec((1, capacity, tile), functools.partial(place, quarter, d))
        for quarter in range(4)
        for d in range(count)
    ]
    shape = jax.ShapeDtypeStruct((2 * count * capacity, width), rows.dtype)
    return pl.pallas_call(
        functools.partial(pack_kernel, count),
        grid_spec=pltpu.PrefetchScalarGridSpec(
            num_scalar_prefetch=1,
            grid=(2, width // tile),
            in_specs=in_specs,
            out_specs=[pl.BlockSpec((count * capacity, tile), lambda g, j, me_ref: (g, j))] * 4,
        ),
        out_shape=[shape] * 4,
        compiler_params=pltpu.CompilerParams(vmem_limit_bytes=VMEM_LIMIT),
        cost_estimate=pl.CostEstimate(
            flops=0, bytes_accessed=4 * devices * capacity * width, transcendentals=0
        ),
        name="pack_rows",
    )(me, *([rows] * (4 * count)))


def weights_kernel(count, capacity, first, me_ref, routes_ref, out_ref):
    step = pl.program_id(0)
    tokens = routes_ref.shape[2]
    topk = routes_ref.shape[1] // 2
    ids = routes_ref[0, :topk, :]
    gates = routes_ref[0, topk:, :]
    scaled = ROUTE_SCALE * gates / jnp.sum(gates, axis=0, keepdims=True)
    before = lax.broadcasted_iota(jnp.int32, (tokens, tokens), 0) < lax.broadcasted_iota(
        jnp.int32, (tokens, tokens), 1
    )
    before = jnp.where(before, 1.0, 0.0).astype(jnp.bfloat16)
    row = lax.broadcasted_iota(jnp.int32, (count * capacity, tokens), 0)
    row = row - lax.rem(step, count) * capacity
    row = row.astype(jnp.float32)
    for source in range(4):
        owner = me_ref[0] ^ ((source & 1) ^ (first if source & 2 else 0))
        low = (owner * EXP_DEV).astype(jnp.float32)
        match = jnp.where((ids >= low) & (ids < low + EXP_DEV), 1.0, 0.0)
        per_token = jnp.broadcast_to(jnp.sum(match, axis=0, keepdims=True), match.shape)
        prior = jnp.dot(
            per_token.astype(jnp.bfloat16), before, preferred_element_type=jnp.float32
        )
        slot = prior[0:1, :]
        total = jnp.zeros((count * capacity, tokens), jnp.float32)
        for k in range(topk):
            weight = scaled[k : k + 1, :] * match[k : k + 1, :]
            total = total + jnp.where(row == slot, weight, 0.0)
            slot = slot + match[k : k + 1, :]
        out_ref[0, source, :, :] = total.T.astype(jnp.bfloat16)


def combine_weights(me, routes, capacity, first, rest):
    devices, lines, tokens = routes.shape
    count = devices // 8

    def place(i, me_ref):
        index = me_ref[0]
        for bit, mask in enumerate(reversed(rest)):
            index = index ^ (((i >> bit) & 1) * mask)
        return (index, 0, 0)

    return pl.pallas_call(
        functools.partial(weights_kernel, count, capacity, first),
        grid_spec=pltpu.PrefetchScalarGridSpec(
            num_scalar_prefetch=1,
            grid=(2 * count,),
            in_specs=[pl.BlockSpec((1, lines, tokens), place)],
            out_specs=pl.BlockSpec(
                (1, 4, tokens, count * capacity),
                lambda i, me_ref: (i // count, 0, lax.rem(i, count), 0),
            ),
        ),
        out_shape=jax.ShapeDtypeStruct(
            (2, 4, count * tokens, count * capacity), jnp.bfloat16
        ),
        compiler_params=pltpu.CompilerParams(vmem_limit_bytes=VMEM_LIMIT),
        name="combine_weights",
    )(me, routes)


def weigh(weights_ref, row_refs):
    total = None
    for source, ref in enumerate(row_refs):
        part = jnp.dot(weights_ref[0, source], ref[...], preferred_element_type=jnp.float32)
        total = part if total is None else total + part
    return total


def send_kernel(weights_ref, a, b, c, d, out_ref):
    out_ref[...] = weigh(weights_ref, (a, b, c, d)).astype(out_ref.dtype)


def keep_kernel(weights_ref, a, b, c, d, got_ref, keep_ref, send_ref):
    total = weigh(weights_ref, (a, b, c, d)) + got_ref[...].astype(jnp.float32)
    half = keep_ref.shape[0]
    keep_ref[...] = total[:half].astype(keep_ref.dtype)
    send_ref[...] = total[half:].astype(send_ref.dtype)


def matmul_call(weights, rows, got, group):
    _, sources, out_rows, depth = weights.shape
    width = rows[0].shape[1]
    tile = 512 if width % 512 == 0 else 256
    in_specs = [pl.BlockSpec((1, sources, out_rows, depth), lambda j: (group, 0, 0, 0))]
    in_specs += [pl.BlockSpec((depth, tile), lambda j: (group, j))] * 4
    whole = pl.BlockSpec((out_rows, tile), lambda j: (0, j))
    half = pl.BlockSpec((out_rows // 2, tile), lambda j: (0, j))
    if got is None:
        kernel, extra, out_specs = send_kernel, (), whole
        out_shape = jax.ShapeDtypeStruct((out_rows, width), jnp.bfloat16)
    else:
        kernel, extra, out_specs = keep_kernel, (got,), [half, half]
        out_shape = [jax.ShapeDtypeStruct((out_rows // 2, width), jnp.bfloat16)] * 2
        in_specs.append(whole)
    return pl.pallas_call(
        kernel,
        grid=(width // tile,),
        in_specs=in_specs,
        out_specs=out_specs,
        out_shape=out_shape,
        compiler_params=pltpu.CompilerParams(vmem_limit_bytes=VMEM_LIMIT),
        cost_estimate=pl.CostEstimate(
            flops=2 * sources * out_rows * depth * width,
            bytes_accessed=2 * width * (sources * depth + 2 * out_rows),
            transcendentals=0,
        ),
        name="partial_sums",
    )(weights, *rows, *extra)


def attention_kernel(
    scale, key_index, query_block, queries_ref, key_up_ref, value_up_ref, *refs
):
    blocks = len(refs) - 4
    keys, out_ref = refs[:blocks], refs[blocks]
    scores_ref, total_ref, weight_ref = refs[blocks + 1 :]
    block_len = queries_ref.shape[0]
    place = query_block[pl.program_id(0)]
    queries = queries_ref[...]
    absorbed = jnp.dot(
        queries[:, :PLAIN_HEAD_WIDTH], key_up_ref[...], preferred_element_type=jnp.float32
    ).astype(jnp.bfloat16)
    rotary = queries[:, PLAIN_HEAD_WIDTH:]
    contract = (((1,), (1,)), ((), ()))
    ahead = lax.broadcasted_iota(jnp.int32, (block_len, block_len), 1) > lax.broadcasted_iota(
        jnp.int32, (block_len, block_len), 0
    )

    def scores_of(j):
        plain = lax.dot_general(
            absorbed, keys[j][:, :LATENT_WIDTH], contract, preferred_element_type=jnp.float32
        )
        turned = lax.dot_general(
            rotary, keys[j][:, LATENT_WIDTH:], contract, preferred_element_type=jnp.float32
        )
        return (plain + turned) * scale

    total_ref[...] = jnp.full(total_ref.shape, -1e30, jnp.float32)
    lanes = total_ref.shape[1]

    def lane_max(values):
        best = total_ref[...]
        for i in range(block_len // lanes):
            best = jnp.maximum(best, values[:, i * lanes : (i + 1) * lanes])
        total_ref[...] = best

    for j in range(blocks):

        @pl.when(j < place)
        def _():
            scores = scores_of(j)
            scores_ref[j] = scores
            lane_max(scores)

        @pl.when(j == place)
        def _():
            scores = jnp.where(ahead, -1e30, scores_of(j))
            scores_ref[j] = scores
            lane_max(scores)

    row_max = jnp.max(total_ref[...], axis=1, keepdims=True)
    total_ref[...] = jnp.zeros(total_ref.shape, jnp.float32)
    weight_ref[...] = jnp.zeros(weight_ref.shape, jnp.float32)
    for j in range(blocks):

        @pl.when(j <= place)
        def _():
            probs = jnp.exp(scores_ref[j] - row_max)
            some = total_ref[...]
            for i in range(block_len // lanes):
                some = some + probs[:, i * lanes : (i + 1) * lanes]
            total_ref[...] = some
            weight_ref[...] += jnp.dot(
                probs.astype(jnp.bfloat16),
                keys[j][:, :LATENT_WIDTH],
                preferred_element_type=jnp.float32,
            )

    weight_sum = jnp.sum(total_ref[...], axis=1, keepdims=True)
    latent_out = (weight_ref[...] / weight_sum).astype(jnp.bfloat16)
    out_ref[...] = jnp.dot(
        latent_out, value_up_ref[...], preferred_element_type=jnp.float32
    ).astype(out_ref.dtype)


def attend(queries, keys, key_up, value_up, key_index, query_block, first, count):
    blocks = key_index.shape[0]
    block_len = keys.shape[0] // blocks
    head_width = queries.shape[1]

    def key_place(p, i, key_index, query_block):
        return (key_index[p], 0)

    in_specs = [
        pl.BlockSpec((block_len, head_width), lambda i, a, b: (first + i, 0)),
        pl.BlockSpec(key_up.shape, lambda i, a, b: (0, 0)),
        pl.BlockSpec(value_up.shape, lambda i, a, b: (0, 0)),
    ]
    in_specs += [
        pl.BlockSpec((block_len, keys.shape[1]), functools.partial(key_place, p))
        for p in range(blocks)
    ]
    scale = 1.0 / math.sqrt(PLAIN_HEAD_WIDTH + ROTARY_WIDTH)
    return pl.pallas_call(
        functools.partial(attention_kernel, scale),
        grid_spec=pltpu.PrefetchScalarGridSpec(
            num_scalar_prefetch=2,
            grid=(count,),
            in_specs=in_specs,
            out_specs=pl.BlockSpec((block_len, VALUE_WIDTH), lambda i, a, b: (i, 0)),
            scratch_shapes=[
                pltpu.VMEM((blocks, block_len, block_len), jnp.float32),
                pltpu.VMEM((block_len, 128), jnp.float32),
                pltpu.VMEM((block_len, LATENT_WIDTH), jnp.float32),
            ],
        ),
        out_shape=jax.ShapeDtypeStruct((count * block_len, VALUE_WIDTH), jnp.bfloat16),
        compiler_params=pltpu.CompilerParams(vmem_limit_bytes=VMEM_LIMIT),
        cost_estimate=pl.CostEstimate(
            flops=count * blocks * block_len * block_len * 1100,
            bytes_accessed=2 * keys.size,
            transcendentals=count * blocks * block_len * block_len // 2,
        ),
        name="latent_attention",
    )(key_index, query_block[first : first + count], queries, key_up, value_up, *([keys] * blocks))


def shards(
    queries, latent, key_up_weight, value_up_weight, block_order, expert_ids, gates, expert_rows
):
    n_ctx, n_exp = lax.axis_size("ctx"), lax.axis_size("exp")
    devices = n_ctx * n_exp
    ctx = lax.axis_index("ctx").astype(jnp.int32)
    exp = lax.axis_index("exp").astype(jnp.int32)
    me = (ctx * n_exp + exp).reshape(1)
    capacity, model_width = expert_rows.shape[4:]
    rows = expert_rows.reshape(devices, capacity, model_width)

    local_routes = jnp.concatenate([expert_ids.T.astype(jnp.float32), gates.T], axis=0)
    routes = lax.all_gather(local_routes, AXES, axis=0)

    local_len = latent.shape[0]
    eighth = local_len // 8
    mine = lax.dynamic_slice_in_dim(latent, (exp % 8) * eighth, eighth, axis=0)
    crossed = exchange(mine, n_exp, devices)
    groups = [list(range(i, i + 8)) for i in range(0, n_exp, 8)]
    other = lax.all_gather(crossed, "exp", axis=0, tiled=True, axis_index_groups=groups)
    keys = jnp.concatenate([latent, other], axis=0)

    extra = [1 << b for b in range(4, n_exp.bit_length() - 1)]
    orders = {"x": [n_exp, 2, 4, 8] + extra, "y": [2, n_exp, 4, 8] + extra}
    weights = {
        name: combine_weights(me, routes, capacity, order[0], order[1:])
        for name, order in orders.items()
    }
    pieces = []
    start = 0
    for width, name in CHUNKS:
        order = orders[name]
        first, rest = order[0], order[1:]
        packed = pack(me, rows, start, width, first, rest)
        start += width
        held = [packed[0]]
        for quarter, mask in ((1, 1), (2, first), (3, 1 ^ first)):
            held.append(exchange(packed[quarter], mask, devices))
        got = exchange(matmul_call(weights[name], held, None, 1), rest[0], devices)
        keep, send = matmul_call(weights[name], held, got, 0)
        for mask in rest[1:]:
            got = exchange(send, mask, devices)
            total = keep.astype(jnp.float32) + got.astype(jnp.float32)
            total = total.astype(jnp.bfloat16)
            half = total.shape[0] // 2
            keep, send = total[:half], total[half:]
        pieces.append(total)
    combined = jnp.concatenate(pieces, axis=1)

    blocks = block_order.shape[0]
    local_blocks = blocks // n_ctx
    ids = jnp.arange(blocks, dtype=jnp.int32)
    stored = jnp.sum(jnp.where(block_order[None, :] == ids[:, None], ids[None, :], 0), axis=1)
    key_index = ((stored // local_blocks) ^ ctx) * local_blocks + stored % local_blocks
    query_block = lax.dynamic_slice_in_dim(block_order, ctx * local_blocks, local_blocks)
    heads = key_up_weight.shape[0]
    head_width = PLAIN_HEAD_WIDTH + ROTARY_WIDTH
    per_call = 2
    columns = []
    for h in range(heads):
        head_queries = queries[:, h * head_width : (h + 1) * head_width]
        parts = [
            attend(
                head_queries, keys, key_up_weight[h], value_up_weight[h], key_index, query_block, b, per_call
            )
            for b in range(0, local_blocks, per_call)
        ]
        columns.append(jnp.concatenate(parts, axis=0))
    attended = columns[0] if heads == 1 else jnp.concatenate(columns, axis=1)
    return (attended, combined)


def solution(mesh):
    return jax.shard_map(
        shards,
        mesh=mesh,
        in_specs=(
            P("ctx", "exp"),
            P("ctx", None),
            P("exp", None, None),
            P("exp", None, None),
            P(),
            P(("ctx", "exp"), None),
            P(("ctx", "exp"), None),
            P("ctx", "exp", None, None, None, None),
        ),
        out_specs=(P("ctx", "exp"), P(("ctx", "exp"), None)),
        check_vma=False,
    )
```

```python
import functools
import math

import jax
import jax.numpy as jnp
from jax import lax
from jax.experimental import pallas as pl
from jax.experimental.pallas import tpu as pltpu
from jax.sharding import PartitionSpec as P

LATENT_WIDTH = 512
PLAIN_HEAD_WIDTH = 128
ROTARY_WIDTH = 64
VALUE_WIDTH = 128
EXP_DEV = 3
ROUTE_SCALE = 2.827
AXES = ("ctx", "exp")
VMEM_LIMIT = 60 * 1024 * 1024
SMALL = pl.CostEstimate(flops=0, bytes_accessed=0, transcendentals=0)
LARGE = pl.CostEstimate(flops=10**12, bytes_accessed=0, transcendentals=0)

STEPS = ((768, True), (1536, True), (1792, True), (1536, True), (1024, False), (512, False))
QUERY_BLOCKS = (0, 3, 3, 2, 0, 0)
LONG_PACKS = (1, 2)
SENDS = (4, 2, 5, 3, 1, 6, 7)
IN_FLIGHT = 5


def after(value, *others):
    return lax.optimization_barrier((value, *others))[0]


def exchange(value, mask, devices):
    return lax.ppermute(value, AXES, [(i, i ^ mask) for i in range(devices)])


def tile_of(start, width):
    for tile in (512, 256, 128):
        if start % tile == 0 and width % tile == 0:
            return tile
    raise ValueError("columns")


def pack_kernel(ctx_ref, select_ref, near_ref, far_ref, *outs):
    for far, ref in enumerate((near_ref, far_ref)):
        rows = jnp.dot(select_ref[...], ref[0], preferred_element_type=jnp.float32)
        lines = rows.shape[0] // 4
        for q in range(4):
            outs[4 * far + q][...] = rows[q * lines : (q + 1) * lines].astype(jnp.bfloat16)


def pack(ctx, select, rows, start, width, long):
    depth = rows.shape[1]
    tile = tile_of(start, width)
    block = start // tile
    return pl.pallas_call(
        pack_kernel,
        grid_spec=pltpu.PrefetchScalarGridSpec(
            num_scalar_prefetch=1,
            grid=(width // tile,),
            in_specs=[
                pl.BlockSpec((depth, depth), lambda j, ctx: (0, 0)),
                pl.BlockSpec((1, depth, tile), lambda j, ctx: (ctx[0], 0, block + j)),
                pl.BlockSpec((1, depth, tile), lambda j, ctx: (1 - ctx[0], 0, block + j)),
            ],
            out_specs=[pl.BlockSpec((depth // 4, tile), lambda j, ctx: (0, j))] * 8,
        ),
        out_shape=[jax.ShapeDtypeStruct((depth // 4, width), rows.dtype)] * 8,
        compiler_params=pltpu.CompilerParams(vmem_limit_bytes=VMEM_LIMIT),
        cost_estimate=LARGE if long else SMALL,
        name="pack_rows",
    )(ctx, select, rows, rows)


def weights_kernel(count, capacity, across, me_ref, routes_ref, out_ref):
    tokens = routes_ref.shape[2]
    topk = routes_ref.shape[1] // 2
    ids = routes_ref[0, :topk, :]
    gates = routes_ref[0, topk:, :]
    scaled = ROUTE_SCALE * gates / jnp.sum(gates, axis=0, keepdims=True)
    before = lax.broadcasted_iota(jnp.int32, (tokens, tokens), 0) < lax.broadcasted_iota(
        jnp.int32, (tokens, tokens), 1
    )
    before = jnp.where(before, 1.0, 0.0).astype(jnp.bfloat16)
    row = lax.broadcasted_iota(jnp.int32, (count * capacity, tokens), 0)
    row = (row - pl.program_id(0) * capacity).astype(jnp.float32)
    totals = []
    for source in range(8):
        owner = me_ref[0] ^ ((source & 3) | (across if source & 4 else 0))
        low = (owner * EXP_DEV).astype(jnp.float32)
        match = jnp.where((ids >= low) & (ids < low + EXP_DEV), 1.0, 0.0)
        per_token = jnp.broadcast_to(jnp.sum(match, axis=0, keepdims=True), match.shape)
        prior = jnp.dot(
            per_token.astype(jnp.bfloat16), before, preferred_element_type=jnp.float32
        )
        slot = prior[0:1, :]
        total = jnp.zeros((count * capacity, tokens), jnp.float32)
        for k in range(topk):
            weight = scaled[k : k + 1, :] * match[k : k + 1, :]
            total = total + jnp.where(row == slot, weight, 0.0)
            slot = slot + match[k : k + 1, :]
        totals.append(total)
    out_ref[...] = jnp.concatenate(totals, axis=0).T.astype(jnp.bfloat16)


def combine_weights(me, routes, capacity, across):
    count, lines, tokens = routes.shape

    def place(i, me_ref):
        return (i ^ ((me_ref[0] >> 2) & (count - 1)), 0, 0)

    return pl.pallas_call(
        functools.partial(weights_kernel, count, capacity, across),
        grid_spec=pltpu.PrefetchScalarGridSpec(
            num_scalar_prefetch=1,
            grid=(count,),
            in_specs=[pl.BlockSpec((1, lines, tokens), place)],
            out_specs=pl.BlockSpec((tokens, 8 * count * capacity), lambda i, me_ref: (i, 0)),
        ),
        out_shape=jax.ShapeDtypeStruct((count * tokens, 8 * count * capacity), jnp.bfloat16),
        compiler_params=pltpu.CompilerParams(vmem_limit_bytes=VMEM_LIMIT),
        cost_estimate=SMALL,
        name="combine_weights",
    )(me, routes)


def sums_kernel(tokens, side_ref, weights_ref, *refs):
    rows = jnp.concatenate([ref[...] for ref in refs[:8]], axis=0)
    total = jnp.dot(weights_ref[...], rows, preferred_element_type=jnp.float32)
    outs = refs[8:]
    if len(outs) == 1:
        outs[0][...] = total.astype(outs[0].dtype)
        return
    first = side_ref[0] == 0
    for pair in range(total.shape[0] // (2 * tokens)):
        even = total[2 * pair * tokens : (2 * pair + 1) * tokens]
        odd = total[(2 * pair + 1) * tokens : (2 * pair + 2) * tokens]
        here = slice(pair * tokens, (pair + 1) * tokens)
        outs[0][here, :] = jnp.where(first, even, odd).astype(outs[0].dtype)
        outs[1][here, :] = jnp.where(first, odd, even).astype(outs[1].dtype)


def partial_sums(weights, rows, side, tokens, split):
    out_rows, depth = weights.shape
    width = rows[0].shape[1]
    tile = tile_of(0, width)
    parts = 2 if split else 1
    return pl.pallas_call(
        functools.partial(sums_kernel, tokens),
        grid_spec=pltpu.PrefetchScalarGridSpec(
            num_scalar_prefetch=1,
            grid=(width // tile,),
            in_specs=[pl.BlockSpec((out_rows, depth), lambda j, side: (0, 0))]
            + [pl.BlockSpec((depth // 8, tile), lambda j, side: (0, j))] * 8,
            out_specs=[pl.BlockSpec((out_rows // parts, tile), lambda j, side: (0, j))] * parts,
        ),
        out_shape=[jax.ShapeDtypeStruct((out_rows // parts, width), jnp.bfloat16)] * parts,
        compiler_params=pltpu.CompilerParams(vmem_limit_bytes=VMEM_LIMIT),
        cost_estimate=SMALL,
        name="partial_sums",
    )(side, weights, *rows)


def attention_kernel(
    scale, first, info, queries_ref, key_up_ref, value_up_ref, own_ref, other_ref, out_ref,
    keys_ref, full_ref, scores_ref, lane_ref, weight_ref, sems,
):
    blocks = sems.shape[0]
    block_len = queries_ref.shape[0]
    step = pl.program_id(0)
    tile = scores_ref.shape[2]
    lanes = lane_ref.shape[1]

    def copy_of(p, source):
        begin = pl.multiple_of(info[1 + blocks + p] * block_len, block_len)
        return pltpu.make_async_copy(
            source.at[pl.ds(begin, block_len)],
            keys_ref.at[pl.ds(pl.multiple_of(p * block_len, block_len), block_len)],
            sems.at[p],
        )

    @pl.when(step == 0)
    def _():
        for p in range(blocks):
            pl.when(info[1 + p] == info[0])(lambda: copy_of(p, own_ref).start())
            pl.when(info[1 + p] != info[0])(lambda: copy_of(p, other_ref).start())

    queries = queries_ref[...]
    full_ref[:, :LATENT_WIDTH] = jnp.dot(
        queries[:, :PLAIN_HEAD_WIDTH], key_up_ref[...], preferred_element_type=jnp.float32
    ).astype(jnp.bfloat16)
    full_ref[:, LATENT_WIDTH:] = queries[:, PLAIN_HEAD_WIDTH:]

    place = info[1 + 2 * blocks + first + step]
    last = place * block_len // tile

    def wait_for(t):
        @pl.when(step == 0)
        def _():
            for p in range(tile // block_len):
                copy_of(t * (tile // block_len) + p, own_ref).wait()
    factor = scale * math.log2(math.e)

    def keys_of(t):
        return keys_ref[pl.ds(pl.multiple_of(t * tile, tile), tile), :]

    def lane_parts(values):
        return [values[:, i * lanes : (i + 1) * lanes] for i in range(tile // lanes)]

    def score(t, masked):
        scores = lax.dot_general(
            full_ref[...], keys_of(t), (((1,), (1,)), ((), ())), preferred_element_type=jnp.float32
        )
        if masked:
            key = lax.broadcasted_iota(jnp.int32, scores.shape, 1) + t * tile
            query = lax.broadcasted_iota(jnp.int32, scores.shape, 0) + place * block_len
            scores = jnp.where(key <= query, scores, -1e30)
        scores_ref[t] = scores
        lane_ref[...] = functools.reduce(jnp.maximum, lane_parts(scores), lane_ref[...])

    lane_ref[...] = jnp.full(lane_ref.shape, -1e30, jnp.float32)

    @pl.loop(0, last)
    def _(t):
        wait_for(t)
        score(t, False)

    wait_for(last)
    score(last, True)
    highest = jnp.max(lane_ref[...], axis=1, keepdims=True) * factor
    lane_ref[...] = jnp.zeros(lane_ref.shape, jnp.float32)
    weight_ref[...] = jnp.zeros(weight_ref.shape, jnp.float32)

    @pl.loop(0, last + 1)
    def _(t):
        probs = jnp.exp2(scores_ref[t] * factor - highest)
        lane_ref[...] = functools.reduce(jnp.add, lane_parts(probs), lane_ref[...])
        weight_ref[...] += jnp.dot(
            probs.astype(jnp.bfloat16),
            keys_of(t)[:, :LATENT_WIDTH],
            preferred_element_type=jnp.float32,
        )

    weight_sum = jnp.sum(lane_ref[...], axis=1, keepdims=True)
    latent_out = (weight_ref[...] / weight_sum).astype(jnp.bfloat16)
    out_ref[...] = jnp.dot(
        latent_out, value_up_ref[...], preferred_element_type=jnp.float32
    ).astype(out_ref.dtype)

    @pl.loop(last + 1, scores_ref.shape[0])
    def _(t):
        wait_for(t)


def attend(queries, own, other, key_up, value_up, info, blocks, first, count):
    block_len = 2 * own.shape[0] // blocks
    head_width = queries.shape[1]
    tile = 2 * block_len
    hbm = pl.BlockSpec(memory_space=pl.ANY)
    return pl.pallas_call(
        functools.partial(
            attention_kernel, 1.0 / math.sqrt(PLAIN_HEAD_WIDTH + ROTARY_WIDTH), first
        ),
        grid_spec=pltpu.PrefetchScalarGridSpec(
            num_scalar_prefetch=1,
            grid=(count,),
            in_specs=[
                pl.BlockSpec((block_len, head_width), lambda i, info: (first + i, 0)),
                pl.BlockSpec(key_up.shape, lambda i, info: (0, 0)),
                pl.BlockSpec(value_up.shape, lambda i, info: (0, 0)),
                hbm,
                hbm,
            ],
            out_specs=pl.BlockSpec((block_len, VALUE_WIDTH), lambda i, info: (i, 0)),
            scratch_shapes=[
                pltpu.VMEM((blocks * block_len, own.shape[1]), jnp.bfloat16),
                pltpu.VMEM((block_len, own.shape[1]), jnp.bfloat16),
                pltpu.VMEM((blocks * block_len // tile, block_len, tile), jnp.float32),
                pltpu.VMEM((block_len, 128), jnp.float32),
                pltpu.VMEM((block_len, LATENT_WIDTH), jnp.float32),
                pltpu.SemaphoreType.DMA((blocks,)),
            ],
        ),
        out_shape=jax.ShapeDtypeStruct((count * block_len, VALUE_WIDTH), jnp.bfloat16),
        compiler_params=pltpu.CompilerParams(vmem_limit_bytes=VMEM_LIMIT),
        cost_estimate=LARGE,
        name="latent_attention",
    )(info, queries, key_up, value_up, own, other)


def shards(
    queries, latent, key_up_weight, value_up_weight, block_order, expert_ids, gates, expert_rows
):
    n_ctx, n_exp = lax.axis_size("ctx"), lax.axis_size("exp")
    devices = n_ctx * n_exp
    ctx = lax.axis_index("ctx").astype(jnp.int32)
    exp = lax.axis_index("exp").astype(jnp.int32)
    me = (ctx * n_exp + exp).reshape(1)
    capacity, model_width = expert_rows.shape[4:]
    rows = jnp.transpose(expert_rows[0, 0], (0, 2, 1, 3)).reshape(n_ctx, capacity * n_exp, model_width)
    count = n_exp // 4
    slots = jnp.arange(n_exp * capacity, dtype=jnp.int32)
    relative = slots // (count * capacity)
    low_bits = (exp & 3) ^ relative
    wanted = (slots % capacity) * n_exp + (slots // capacity) % count * 4 + low_bits
    select = (wanted[:, None] == slots[None, :]).astype(jnp.bfloat16)

    ctx1, side = ctx.reshape(1), ((exp >> 2) & 1).reshape(1)
    steps, tokens = len(STEPS), expert_ids.shape[0]
    packed, held, sent = [None] * steps, [[None] * 8 for _ in STEPS], []

    def pack_step(i, *others):
        start = sum(width for width, _ in STEPS[:i])
        return pack(after(ctx1, *others), select, rows, start, STEPS[i][0], i in LONG_PACKS)

    def send(i, parts, *others):
        for part in parts:
            mask = (part & 3) | (n_exp if part & 4 else 0)
            queue = sent[-IN_FLIGHT : 1 - IN_FLIGHT]
            held[i][part] = exchange(after(packed[i][part], *queue, *others), mask, devices)
            sent.append(held[i][part])

    packed[0] = pack_step(0)

    routes = jnp.concatenate([expert_ids.T.astype(jnp.float32), gates.T], axis=0)[None]
    routes = after(routes, packed[0][0])
    for bit in range(2, n_exp.bit_length() - 1):
        routes = jnp.concatenate([routes, exchange(routes, 1 << bit, devices)], axis=0)
    send(0, SENDS[:4])
    packed[1] = pack_step(1, packed[0][0])
    weights = combine_weights(after(me, packed[1][0]), routes, capacity, n_exp)
    send(0, SENDS[4:])
    send(1, SENDS[:4])
    last = [weights]

    latent = after(latent, packed[1][0])
    members = n_exp // 2
    share = latent.shape[0] // members
    place = (exp >> 2) * 2 + (exp & 1)
    mine = lax.dynamic_slice_in_dim(latent, place * share, share, axis=0)
    part = exchange(after(mine, *sent[:2]), n_exp, devices)
    groups = [[d for d in range(n_exp) if (d >> 1) & 1 == bit] for bit in range(2)]
    other = lax.all_gather(
        after(part, *sent[4:7]), "exp", axis=0, tiled=True, axis_index_groups=groups
    )

    blocks = block_order.shape[0]
    local_blocks = blocks // n_ctx
    ids = jnp.arange(blocks, dtype=jnp.int32)
    stored = jnp.sum(jnp.where(block_order[None, :] == ids[:, None], ids[None, :], 0), axis=1)
    query_block = lax.dynamic_slice_in_dim(block_order, ctx * local_blocks, local_blocks)
    info = jnp.concatenate([ctx1, stored // local_blocks, stored % local_blocks, query_block])
    heads = key_up_weight.shape[0]
    head_width = PLAIN_HEAD_WIDTH + ROTARY_WIDTH
    outputs, done_blocks = [], 0

    def attention_part(count, *last):
        nonlocal done_blocks
        part = []
        for h in range(heads):
            head_queries = queries[:, h * head_width : (h + 1) * head_width]
            part.append(
                attend(
                    head_queries,
                    latent,
                    other,
                    key_up_weight[h],
                    value_up_weight[h],
                    after(info, *last),
                    blocks,
                    done_blocks,
                    count,
                )
            )
        done_blocks += count
        outputs.append(part[0] if heads == 1 else jnp.concatenate(part, axis=1))
        return outputs[-1]

    def halve(total, bit):
        place = (exp >> bit) & 1
        pairs = total.reshape(-1, 2, tokens, total.shape[1])
        halves = (lax.dynamic_index_in_dim(pairs, p, 1, keepdims=False) for p in (place, 1 - place))
        return [half.reshape(-1, total.shape[1]) for half in halves]

    bits = range(2, n_exp.bit_length() - 1)
    halves = [None] * steps
    pieces = [None] * steps

    def begin(i, keep, send, bit, *others):
        halves[i] = (keep, exchange(after(send, *others), 1 << bit, devices), bit)

    def advance(i, *others):
        keep, got, bit = halves[i]
        keep = after(keep, *others)
        total = (keep.astype(jnp.float32) + got.astype(jnp.float32)).astype(jnp.bfloat16)
        if bit == bits[-1]:
            pieces[i] = total
        else:
            begin(i, *halve(total, bit + 1), bit + 1)

    axis_groups = [list(range(low, n_exp, 4)) for low in range(4)]
    for i, (_, scattered) in enumerate(STEPS):
        held[i][0] = packed[i][0]
        ready = [part] if i == 0 else []
        sums = partial_sums(weights, held[i], after(side, *last, *ready), tokens, not scattered)
        last = sums[:1]
        if i + 1 < steps:
            send(i + 1, SENDS[4:], *last)
        if QUERY_BLOCKS[i]:
            last = [attention_part(QUERY_BLOCKS[i], *last, pieces[i - 1])]
        if i + 2 < steps:
            packed[i + 2] = pack_step(i + 2, *last)
            last = packed[i + 2][:1]
            send(i + 2, SENDS[:4])
        if not scattered:
            begin(i, *sums, bits[0])
        else:
            pieces[i] = lax.psum_scatter(
                after(sums[0], held[i + 1][SENDS[0]], held[i + 1][SENDS[1]]),
                "exp",
                scatter_dimension=0,
                axis_index_groups=axis_groups,
                tiled=True,
            )
    pieces = [piece if piece is None else after(piece, *last) for piece in pieces]
    while any(piece is None for piece in pieces):
        before = ()
        for i in range(steps):
            if pieces[i] is None:
                advance(i, *before)
                before = (halves[i][0] if pieces[i] is None else pieces[i],)
    combined = jnp.concatenate(pieces, axis=1)
    attended = jnp.concatenate(outputs, axis=0)
    return (attended, combined)


def solution(mesh):
    return jax.shard_map(
        shards,
        mesh=mesh,
        in_specs=(
            P("ctx", "exp"),
            P("ctx", None),
            P("exp", None, None),
            P("exp", None, None),
            P(),
            P(("ctx", "exp"), None),
            P(("ctx", "exp"), None),
            P("ctx", "exp", None, None, None, None),
        ),
        out_specs=(P("ctx", "exp"), P(("ctx", "exp"), None)),
        check_vma=False,
    )
```

```python
import functools
import math

import jax
import jax.numpy as jnp
from jax import lax
from jax.experimental import pallas as pl
from jax.experimental.pallas import tpu as pltpu
from jax.sharding import PartitionSpec as P

LATENT_WIDTH = 512
PLAIN_HEAD_WIDTH = 128
ROTARY_WIDTH = 64
VALUE_WIDTH = 128
EXP_DEV = 3
ROUTE_SCALE = 2.827
AXES = ("ctx", "exp")
VMEM_LIMIT = 60 * 1024 * 1024
SMALL = pl.CostEstimate(flops=0, bytes_accessed=0, transcendentals=0)
LARGE = pl.CostEstimate(flops=10**12, bytes_accessed=0, transcendentals=0)

STEPS = ((1024, True), (1536, True), (1536, True), (1536, True), (1024, False), (512, False))
QUERY_BLOCKS = (0, 2, 3, 3, 0, 0)
AHEAD = ((2, 3), (4,), (5,), (), (), ())
LONG_PACKS = (1, 2)
SENDS = (4, 2, 5, 3, 1, 6, 7)
IN_FLIGHT = 6


def after(value, *others):
    return lax.optimization_barrier((value, *others))[0]


def exchange(value, mask, devices):
    return lax.ppermute(value, AXES, [(i, i ^ mask) for i in range(devices)])


def tile_of(start, width):
    for tile in (768, 512, 256, 128):
        if start % tile == 0 and width % tile == 0:
            return tile
    raise ValueError("columns")


def pack_kernel(ctx_ref, select_ref, near_ref, far_ref, *outs):
    for far, ref in enumerate((near_ref, far_ref)):
        rows = jnp.dot(select_ref[...], ref[0], preferred_element_type=jnp.float32)
        lines = rows.shape[0] // 4
        for q in range(4):
            outs[4 * far + q][...] = rows[q * lines : (q + 1) * lines].astype(jnp.bfloat16)


def pack(ctx, select, rows, start, width, long):
    depth = rows.shape[1]
    tile = tile_of(start, width)
    block = start // tile
    return pl.pallas_call(
        pack_kernel,
        grid_spec=pltpu.PrefetchScalarGridSpec(
            num_scalar_prefetch=1,
            grid=(width // tile,),
            in_specs=[
                pl.BlockSpec((depth, depth), lambda j, ctx: (0, 0)),
                pl.BlockSpec((1, depth, tile), lambda j, ctx: (ctx[0], 0, block + j)),
                pl.BlockSpec((1, depth, tile), lambda j, ctx: (1 - ctx[0], 0, block + j)),
            ],
            out_specs=[pl.BlockSpec((depth // 4, tile), lambda j, ctx: (0, j))] * 8,
        ),
        out_shape=[jax.ShapeDtypeStruct((depth // 4, width), rows.dtype)] * 8,
        compiler_params=pltpu.CompilerParams(vmem_limit_bytes=VMEM_LIMIT),
        cost_estimate=LARGE if long else SMALL,
        name="pack_rows",
    )(ctx, select, rows, rows)


def weights_kernel(count, capacity, across, me_ref, routes_ref, out_ref):
    tokens = routes_ref.shape[2]
    topk = routes_ref.shape[1] // 2
    ids = routes_ref[0, :topk, :]
    gates = routes_ref[0, topk:, :]
    scaled = ROUTE_SCALE * gates / jnp.sum(gates, axis=0, keepdims=True)
    before = lax.broadcasted_iota(jnp.int32, (tokens, tokens), 0) < lax.broadcasted_iota(
        jnp.int32, (tokens, tokens), 1
    )
    before = jnp.where(before, 1.0, 0.0).astype(jnp.bfloat16)
    row = lax.broadcasted_iota(jnp.int32, (count * capacity, tokens), 0)
    row = (row - pl.program_id(0) * capacity).astype(jnp.float32)
    totals = []
    for source in range(8):
        owner = me_ref[0] ^ ((source & 3) | (across if source & 4 else 0))
        low = (owner * EXP_DEV).astype(jnp.float32)
        match = jnp.where((ids >= low) & (ids < low + EXP_DEV), 1.0, 0.0)
        per_token = jnp.broadcast_to(jnp.sum(match, axis=0, keepdims=True), match.shape)
        prior = jnp.dot(
            per_token.astype(jnp.bfloat16), before, preferred_element_type=jnp.float32
        )
        slot = prior[0:1, :]
        total = jnp.zeros((count * capacity, tokens), jnp.float32)
        for k in range(topk):
            weight = scaled[k : k + 1, :] * match[k : k + 1, :]
            total = total + jnp.where(row == slot, weight, 0.0)
            slot = slot + match[k : k + 1, :]
        totals.append(total)
    out_ref[...] = jnp.concatenate(totals, axis=0).T.astype(jnp.bfloat16)


def combine_weights(me, routes, capacity, across):
    count, lines, tokens = routes.shape

    def place(i, me_ref):
        return (i ^ ((me_ref[0] >> 2) & (count - 1)), 0, 0)

    return pl.pallas_call(
        functools.partial(weights_kernel, count, capacity, across),
        grid_spec=pltpu.PrefetchScalarGridSpec(
            num_scalar_prefetch=1,
            grid=(count,),
            in_specs=[pl.BlockSpec((1, lines, tokens), place)],
            out_specs=pl.BlockSpec((tokens, 8 * count * capacity), lambda i, me_ref: (i, 0)),
        ),
        out_shape=jax.ShapeDtypeStruct((count * tokens, 8 * count * capacity), jnp.bfloat16),
        compiler_params=pltpu.CompilerParams(vmem_limit_bytes=VMEM_LIMIT),
        cost_estimate=SMALL,
        name="combine_weights",
    )(me, routes)


def sums_kernel(tokens, side_ref, weights_ref, *refs):
    rows = jnp.concatenate([ref[...] for ref in refs[:8]], axis=0)
    total = jnp.dot(weights_ref[...], rows, preferred_element_type=jnp.float32)
    outs = refs[8:]
    if len(outs) == 1:
        outs[0][...] = total.astype(outs[0].dtype)
        return
    first = side_ref[0] == 0
    for pair in range(total.shape[0] // (2 * tokens)):
        even = total[2 * pair * tokens : (2 * pair + 1) * tokens]
        odd = total[(2 * pair + 1) * tokens : (2 * pair + 2) * tokens]
        here = slice(pair * tokens, (pair + 1) * tokens)
        outs[0][here, :] = jnp.where(first, even, odd).astype(outs[0].dtype)
        outs[1][here, :] = jnp.where(first, odd, even).astype(outs[1].dtype)


def partial_sums(weights, rows, side, tokens, split):
    out_rows, depth = weights.shape
    width = rows[0].shape[1]
    tile = tile_of(0, width)
    parts = 2 if split else 1
    return pl.pallas_call(
        functools.partial(sums_kernel, tokens),
        grid_spec=pltpu.PrefetchScalarGridSpec(
            num_scalar_prefetch=1,
            grid=(width // tile,),
            in_specs=[pl.BlockSpec((out_rows, depth), lambda j, side: (0, 0))]
            + [pl.BlockSpec((depth // 8, tile), lambda j, side: (0, j))] * 8,
            out_specs=[pl.BlockSpec((out_rows // parts, tile), lambda j, side: (0, j))] * parts,
        ),
        out_shape=[jax.ShapeDtypeStruct((out_rows // parts, width), jnp.bfloat16)] * parts,
        compiler_params=pltpu.CompilerParams(vmem_limit_bytes=VMEM_LIMIT),
        cost_estimate=SMALL,
        name="partial_sums",
    )(side, weights, *rows)


def attention_kernel(
    scale, first, info, queries_ref, key_up_ref, value_up_ref, own_ref, other_ref, out_ref,
    keys_ref, full_ref, scores_ref, lane_ref, weight_ref, sems,
):
    blocks = sems.shape[0]
    block_len = queries_ref.shape[0]
    step = pl.program_id(0)
    tile = scores_ref.shape[2]
    lanes = lane_ref.shape[1]

    def copy_of(p, source):
        begin = pl.multiple_of(info[1 + blocks + p] * block_len, block_len)
        return pltpu.make_async_copy(
            source.at[pl.ds(begin, block_len)],
            keys_ref.at[pl.ds(pl.multiple_of(p * block_len, block_len), block_len)],
            sems.at[p],
        )

    @pl.when(step == 0)
    def _():
        for p in range(blocks):
            pl.when(info[1 + p] == info[0])(lambda: copy_of(p, own_ref).start())
            pl.when(info[1 + p] != info[0])(lambda: copy_of(p, other_ref).start())

    queries = queries_ref[...]
    full_ref[:, :LATENT_WIDTH] = jnp.dot(
        queries[:, :PLAIN_HEAD_WIDTH], key_up_ref[...], preferred_element_type=jnp.float32
    ).astype(jnp.bfloat16)
    full_ref[:, LATENT_WIDTH:] = queries[:, PLAIN_HEAD_WIDTH:]

    place = info[1 + 2 * blocks + first + step]
    last = place * block_len // tile

    def wait_for(t):
        @pl.when(step == 0)
        def _():
            for p in range(tile // block_len):
                copy_of(t * (tile // block_len) + p, own_ref).wait()
    factor = scale * math.log2(math.e)

    def keys_of(t):
        return keys_ref[pl.ds(pl.multiple_of(t * tile, tile), tile), :]

    def lane_parts(values):
        return [values[:, i * lanes : (i + 1) * lanes] for i in range(tile // lanes)]

    def score(t, masked):
        scores = lax.dot_general(
            full_ref[...], keys_of(t), (((1,), (1,)), ((), ())), preferred_element_type=jnp.float32
        )
        if masked:
            key = lax.broadcasted_iota(jnp.int32, scores.shape, 1) + t * tile
            query = lax.broadcasted_iota(jnp.int32, scores.shape, 0) + place * block_len
            scores = jnp.where(key <= query, scores, -1e30)
        scores_ref[t] = scores
        lane_ref[...] = functools.reduce(jnp.maximum, lane_parts(scores), lane_ref[...])

    lane_ref[...] = jnp.full(lane_ref.shape, -1e30, jnp.float32)

    @pl.loop(0, last)
    def _(t):
        wait_for(t)
        score(t, False)

    wait_for(last)
    score(last, True)
    highest = jnp.max(lane_ref[...], axis=1, keepdims=True) * factor
    lane_ref[...] = jnp.zeros(lane_ref.shape, jnp.float32)
    weight_ref[...] = jnp.zeros(weight_ref.shape, jnp.float32)

    @pl.loop(0, last + 1)
    def _(t):
        probs = jnp.exp2(scores_ref[t] * factor - highest)
        lane_ref[...] = functools.reduce(jnp.add, lane_parts(probs), lane_ref[...])
        weight_ref[...] += jnp.dot(
            probs.astype(jnp.bfloat16),
            keys_of(t)[:, :LATENT_WIDTH],
            preferred_element_type=jnp.float32,
        )

    weight_sum = jnp.sum(lane_ref[...], axis=1, keepdims=True)
    latent_out = (weight_ref[...] / weight_sum).astype(jnp.bfloat16)
    out_ref[...] = jnp.dot(
        latent_out, value_up_ref[...], preferred_element_type=jnp.float32
    ).astype(out_ref.dtype)

    @pl.loop(last + 1, scores_ref.shape[0])
    def _(t):
        wait_for(t)


def attend(queries, own, other, key_up, value_up, info, blocks, first, count):
    block_len = 2 * own.shape[0] // blocks
    head_width = queries.shape[1]
    tile = 2 * block_len
    hbm = pl.BlockSpec(memory_space=pl.ANY)
    return pl.pallas_call(
        functools.partial(
            attention_kernel, 1.0 / math.sqrt(PLAIN_HEAD_WIDTH + ROTARY_WIDTH), first
        ),
        grid_spec=pltpu.PrefetchScalarGridSpec(
            num_scalar_prefetch=1,
            grid=(count,),
            in_specs=[
                pl.BlockSpec((block_len, head_width), lambda i, info: (first + i, 0)),
                pl.BlockSpec(key_up.shape, lambda i, info: (0, 0)),
                pl.BlockSpec(value_up.shape, lambda i, info: (0, 0)),
                hbm,
                hbm,
            ],
            out_specs=pl.BlockSpec((block_len, VALUE_WIDTH), lambda i, info: (i, 0)),
            scratch_shapes=[
                pltpu.VMEM((blocks * block_len, own.shape[1]), jnp.bfloat16),
                pltpu.VMEM((block_len, own.shape[1]), jnp.bfloat16),
                pltpu.VMEM((blocks * block_len // tile, block_len, tile), jnp.float32),
                pltpu.VMEM((block_len, 128), jnp.float32),
                pltpu.VMEM((block_len, LATENT_WIDTH), jnp.float32),
                pltpu.SemaphoreType.DMA((blocks,)),
            ],
        ),
        out_shape=jax.ShapeDtypeStruct((count * block_len, VALUE_WIDTH), jnp.bfloat16),
        compiler_params=pltpu.CompilerParams(vmem_limit_bytes=VMEM_LIMIT),
        cost_estimate=LARGE,
        name="latent_attention",
    )(info, queries, key_up, value_up, own, other)


def shards(
    queries, latent, key_up_weight, value_up_weight, block_order, expert_ids, gates, expert_rows
):
    n_ctx, n_exp = lax.axis_size("ctx"), lax.axis_size("exp")
    devices = n_ctx * n_exp
    ctx = lax.axis_index("ctx").astype(jnp.int32)
    exp = lax.axis_index("exp").astype(jnp.int32)
    me = (ctx * n_exp + exp).reshape(1)
    capacity, model_width = expert_rows.shape[4:]
    rows = jnp.transpose(expert_rows[0, 0], (0, 2, 1, 3)).reshape(n_ctx, capacity * n_exp, model_width)
    count = n_exp // 4
    slots = jnp.arange(n_exp * capacity, dtype=jnp.int32)
    relative = slots // (count * capacity)
    low_bits = (exp & 3) ^ relative
    wanted = (slots % capacity) * n_exp + (slots // capacity) % count * 4 + low_bits
    select = (wanted[:, None] == slots[None, :]).astype(jnp.bfloat16)

    ctx1, side = ctx.reshape(1), ((exp >> 2) & 1).reshape(1)
    steps, tokens = len(STEPS), expert_ids.shape[0]
    packed, held, sent = [None] * steps, [[None] * 8 for _ in STEPS], []

    def pack_step(i, *others):
        start = sum(width for width, _ in STEPS[:i])
        return pack(after(ctx1, *others), select, rows, start, STEPS[i][0], i in LONG_PACKS)

    def send(i, parts, *others):
        for part in parts:
            mask = (part & 3) | (n_exp if part & 4 else 0)
            queue = sent[-IN_FLIGHT : 1 - IN_FLIGHT]
            held[i][part] = exchange(after(packed[i][part], *queue, *others), mask, devices)
            sent.append(held[i][part])

    packed[0] = pack_step(0)

    routes = jnp.concatenate([expert_ids.T.astype(jnp.float32), gates.T], axis=0)[None]
    routes = after(routes, packed[0][0])
    for bit in range(2, n_exp.bit_length() - 1):
        routes = jnp.concatenate([routes, exchange(routes, 1 << bit, devices)], axis=0)
    send(0, SENDS[:4])
    packed[1] = pack_step(1, packed[0][0])
    weights = combine_weights(after(me, packed[1][0]), routes, capacity, n_exp)
    send(0, SENDS[4:])
    send(1, SENDS[:4])
    last = [weights]

    latent = after(latent, packed[1][0])
    members = n_exp // 2
    share = latent.shape[0] // members
    place = (exp >> 2) * 2 + (exp & 1)
    mine = lax.dynamic_slice_in_dim(latent, place * share, share, axis=0)
    part = exchange(after(mine, *sent[:2]), n_exp, devices)
    groups = [[d for d in range(n_exp) if (d >> 1) & 1 == bit] for bit in range(2)]
    other = lax.all_gather(
        after(part, *sent[4:7]), "exp", axis=0, tiled=True, axis_index_groups=groups
    )

    blocks = block_order.shape[0]
    local_blocks = blocks // n_ctx
    ids = jnp.arange(blocks, dtype=jnp.int32)
    stored = jnp.sum(jnp.where(block_order[None, :] == ids[:, None], ids[None, :], 0), axis=1)
    query_block = lax.dynamic_slice_in_dim(block_order, ctx * local_blocks, local_blocks)
    info = jnp.concatenate([ctx1, stored // local_blocks, stored % local_blocks, query_block])
    heads = key_up_weight.shape[0]
    head_width = PLAIN_HEAD_WIDTH + ROTARY_WIDTH
    outputs, done_blocks = [], 0

    def attention_part(count, *last):
        nonlocal done_blocks
        part = []
        for h in range(heads):
            head_queries = queries[:, h * head_width : (h + 1) * head_width]
            part.append(
                attend(
                    head_queries,
                    latent,
                    other,
                    key_up_weight[h],
                    value_up_weight[h],
                    after(info, *last),
                    blocks,
                    done_blocks,
                    count,
                )
            )
        done_blocks += count
        outputs.append(part[0] if heads == 1 else jnp.concatenate(part, axis=1))
        return outputs[-1]

    def halve(total, bit):
        place = (exp >> bit) & 1
        pairs = total.reshape(-1, 2, tokens, total.shape[1])
        halves = (lax.dynamic_index_in_dim(pairs, p, 1, keepdims=False) for p in (place, 1 - place))
        return [half.reshape(-1, total.shape[1]) for half in halves]

    bits = range(2, n_exp.bit_length() - 1)
    halves = [None] * steps
    pieces = [None] * steps

    def begin(i, keep, send, bit, *others):
        halves[i] = (keep, exchange(after(send, *others), 1 << bit, devices), bit)

    def advance(i, *others):
        keep, got, bit = halves[i]
        keep = after(keep, *others)
        total = (keep.astype(jnp.float32) + got.astype(jnp.float32)).astype(jnp.bfloat16)
        if bit == bits[-1]:
            pieces[i] = total
        else:
            begin(i, *halve(total, bit + 1), bit + 1)

    axis_groups = [list(range(low, n_exp, 4)) for low in range(4)]
    for i, (_, scattered) in enumerate(STEPS):
        held[i][0] = packed[i][0]
        ready = [part] if i == 0 else []
        sums = partial_sums(weights, held[i], after(side, *last, *ready), tokens, not scattered)
        last = sums[:1]
        if i + 1 < steps:
            send(i + 1, SENDS[4:], *last)
        if QUERY_BLOCKS[i]:
            last = [attention_part(QUERY_BLOCKS[i], *last, pieces[i - 1])]
        for j in AHEAD[i]:
            packed[j] = pack_step(j, *last)
            last = packed[j][:1]
        if i + 2 < steps:
            send(i + 2, SENDS[:4])
        if not scattered:
            begin(i, *sums, bits[0])
        else:
            pieces[i] = lax.psum_scatter(
                after(sums[0], *[held[i + 1][part] for part in SENDS[: 0 if i else 4]]),
                "exp",
                scatter_dimension=0,
                axis_index_groups=axis_groups,
                tiled=True,
            )
    final = max(i for i, (_, scattered) in enumerate(STEPS) if scattered)
    pieces[final] = after(pieces[final], *last)
    while any(piece is None for piece in pieces):
        before = ()
        for i in range(steps):
            if pieces[i] is None:
                advance(i, *before)
                before = (halves[i][0] if pieces[i] is None else pieces[i],)
    combined = jnp.concatenate(pieces, axis=1)
    attended = jnp.concatenate(outputs, axis=0)
    return (attended, combined)


def solution(mesh):
    return jax.shard_map(
        shards,
        mesh=mesh,
        in_specs=(
            P("ctx", "exp"),
            P("ctx", None),
            P("exp", None, None),
            P("exp", None, None),
            P(),
            P(("ctx", "exp"), None),
            P(("ctx", "exp"), None),
            P("ctx", "exp", None, None, None, None),
        ),
        out_specs=(P("ctx", "exp"), P(("ctx", "exp"), None)),
        check_vma=False,
    )
```

```python
import functools
import math

import jax
import jax.numpy as jnp
from jax import lax
from jax.experimental import pallas as pl
from jax.experimental.pallas import tpu as pltpu
from jax.sharding import PartitionSpec as P

LATENT_WIDTH = 512
PLAIN_HEAD_WIDTH = 128
ROTARY_WIDTH = 64
VALUE_WIDTH = 128
EXP_DEV = 3
ROUTE_SCALE = 2.827
AXES = ("ctx", "exp")
VMEM_LIMIT = 60 * 1024 * 1024
SMALL = pl.CostEstimate(flops=0, bytes_accessed=0, transcendentals=0)
LARGE = pl.CostEstimate(flops=10**12, bytes_accessed=0, transcendentals=0)

STEPS = ((1024, True), (1536, True), (1536, True), (1536, True), (1024, False), (512, False))
QUERY_BLOCKS = (0, 2, 3, 3, 0, 0)
AHEAD = ((2, 3), (4,), (5,), (), (), ())
LONG_PACKS = (1, 2)
SENDS = (4, 2, 5, 3, 1, 7, 6)
IN_FLIGHT = 6


def after(value, *others):
    return lax.optimization_barrier((value, *others))[0]


def exchange(value, mask, devices):
    return lax.ppermute(value, AXES, [(i, i ^ mask) for i in range(devices)])


def tile_of(start, width):
    for tile in (768, 512, 256, 128):
        if start % tile == 0 and width % tile == 0:
            return tile
    raise ValueError("columns")


def pack_kernel(ctx_ref, select_ref, near_ref, far_ref, *outs):
    for far, ref in enumerate((near_ref, far_ref)):
        rows = jnp.dot(select_ref[...], ref[0], preferred_element_type=jnp.float32)
        lines = rows.shape[0] // 4
        for q in range(4):
            outs[4 * far + q][...] = rows[q * lines : (q + 1) * lines].astype(jnp.bfloat16)


def pack(ctx, select, rows, start, width, long):
    depth = rows.shape[1]
    tile = tile_of(start, width)
    block = start // tile
    return pl.pallas_call(
        pack_kernel,
        grid_spec=pltpu.PrefetchScalarGridSpec(
            num_scalar_prefetch=1,
            grid=(width // tile,),
            in_specs=[
                pl.BlockSpec((depth, depth), lambda j, ctx: (0, 0)),
                pl.BlockSpec((1, depth, tile), lambda j, ctx: (ctx[0], 0, block + j)),
                pl.BlockSpec((1, depth, tile), lambda j, ctx: (1 - ctx[0], 0, block + j)),
            ],
            out_specs=[pl.BlockSpec((depth // 4, tile), lambda j, ctx: (0, j))] * 8,
        ),
        out_shape=[jax.ShapeDtypeStruct((depth // 4, width), rows.dtype)] * 8,
        compiler_params=pltpu.CompilerParams(vmem_limit_bytes=VMEM_LIMIT),
        cost_estimate=LARGE if long else SMALL,
        name="pack_rows",
    )(ctx, select, rows, rows)


def weights_kernel(count, capacity, across, me_ref, routes_ref, out_ref):
    tokens = routes_ref.shape[2]
    topk = routes_ref.shape[1] // 2
    ids = routes_ref[0, :topk, :]
    gates = routes_ref[0, topk:, :]
    scaled = ROUTE_SCALE * gates / jnp.sum(gates, axis=0, keepdims=True)
    before = lax.broadcasted_iota(jnp.int32, (tokens, tokens), 0) < lax.broadcasted_iota(
        jnp.int32, (tokens, tokens), 1
    )
    before = jnp.where(before, 1.0, 0.0).astype(jnp.bfloat16)
    row = lax.broadcasted_iota(jnp.int32, (count * capacity, tokens), 0)
    row = (row - pl.program_id(0) * capacity).astype(jnp.float32)
    totals = []
    for source in range(8):
        owner = me_ref[0] ^ ((source & 3) | (across if source & 4 else 0))
        low = (owner * EXP_DEV).astype(jnp.float32)
        match = jnp.where((ids >= low) & (ids < low + EXP_DEV), 1.0, 0.0)
        per_token = jnp.broadcast_to(jnp.sum(match, axis=0, keepdims=True), match.shape)
        prior = jnp.dot(
            per_token.astype(jnp.bfloat16), before, preferred_element_type=jnp.float32
        )
        slot = prior[0:1, :]
        total = jnp.zeros((count * capacity, tokens), jnp.float32)
        for k in range(topk):
            weight = scaled[k : k + 1, :] * match[k : k + 1, :]
            total = total + jnp.where(row == slot, weight, 0.0)
            slot = slot + match[k : k + 1, :]
        totals.append(total)
    out_ref[...] = jnp.concatenate(totals, axis=0).T.astype(jnp.bfloat16)


def combine_weights(me, routes, capacity, across):
    count, lines, tokens = routes.shape

    def place(i, me_ref):
        return (i ^ ((me_ref[0] >> 2) & (count - 1)), 0, 0)

    return pl.pallas_call(
        functools.partial(weights_kernel, count, capacity, across),
        grid_spec=pltpu.PrefetchScalarGridSpec(
            num_scalar_prefetch=1,
            grid=(count,),
            in_specs=[pl.BlockSpec((1, lines, tokens), place)],
            out_specs=pl.BlockSpec((tokens, 8 * count * capacity), lambda i, me_ref: (i, 0)),
        ),
        out_shape=jax.ShapeDtypeStruct((count * tokens, 8 * count * capacity), jnp.bfloat16),
        compiler_params=pltpu.CompilerParams(vmem_limit_bytes=VMEM_LIMIT),
        cost_estimate=SMALL,
        name="combine_weights",
    )(me, routes)


def sums_kernel(tokens, side_ref, weights_ref, *refs):
    rows = jnp.concatenate([ref[...] for ref in refs[:8]], axis=0)
    total = jnp.dot(weights_ref[...], rows, preferred_element_type=jnp.float32)
    outs = refs[8:]
    if len(outs) == 1:
        outs[0][...] = total.astype(outs[0].dtype)
        return
    first = side_ref[0] == 0
    for pair in range(total.shape[0] // (2 * tokens)):
        even = total[2 * pair * tokens : (2 * pair + 1) * tokens]
        odd = total[(2 * pair + 1) * tokens : (2 * pair + 2) * tokens]
        here = slice(pair * tokens, (pair + 1) * tokens)
        outs[0][here, :] = jnp.where(first, even, odd).astype(outs[0].dtype)
        outs[1][here, :] = jnp.where(first, odd, even).astype(outs[1].dtype)


def partial_sums(weights, rows, side, tokens, split):
    out_rows, depth = weights.shape
    width = rows[0].shape[1]
    tile = tile_of(0, width)
    parts = 2 if split else 1
    return pl.pallas_call(
        functools.partial(sums_kernel, tokens),
        grid_spec=pltpu.PrefetchScalarGridSpec(
            num_scalar_prefetch=1,
            grid=(width // tile,),
            in_specs=[pl.BlockSpec((out_rows, depth), lambda j, side: (0, 0))]
            + [pl.BlockSpec((depth // 8, tile), lambda j, side: (0, j))] * 8,
            out_specs=[pl.BlockSpec((out_rows // parts, tile), lambda j, side: (0, j))] * parts,
        ),
        out_shape=[jax.ShapeDtypeStruct((out_rows // parts, width), jnp.bfloat16)] * parts,
        compiler_params=pltpu.CompilerParams(vmem_limit_bytes=VMEM_LIMIT),
        cost_estimate=SMALL,
        name="partial_sums",
    )(side, weights, *rows)


def attention_kernel(
    scale, first, info, queries_ref, key_up_ref, value_up_ref, own_ref, other_ref, out_ref,
    keys_ref, full_ref, scores_ref, lane_ref, weight_ref, sems,
):
    blocks = sems.shape[0]
    block_len = queries_ref.shape[0]
    step = pl.program_id(0)
    tile = scores_ref.shape[2]
    lanes = lane_ref.shape[1]

    def copy_of(p, source):
        begin = pl.multiple_of(info[1 + blocks + p] * block_len, block_len)
        return pltpu.make_async_copy(
            source.at[pl.ds(begin, block_len)],
            keys_ref.at[pl.ds(pl.multiple_of(p * block_len, block_len), block_len)],
            sems.at[p],
        )

    @pl.when(step == 0)
    def _():
        for p in range(blocks):
            pl.when(info[1 + p] == info[0])(lambda: copy_of(p, own_ref).start())
            pl.when(info[1 + p] != info[0])(lambda: copy_of(p, other_ref).start())

    queries = queries_ref[...]
    full_ref[:, :LATENT_WIDTH] = jnp.dot(
        queries[:, :PLAIN_HEAD_WIDTH], key_up_ref[...], preferred_element_type=jnp.float32
    ).astype(jnp.bfloat16)
    full_ref[:, LATENT_WIDTH:] = queries[:, PLAIN_HEAD_WIDTH:]

    place = info[1 + 2 * blocks + first + step]
    last = place * block_len // tile

    def wait_for(t):
        @pl.when(step == 0)
        def _():
            for p in range(tile // block_len):
                copy_of(t * (tile // block_len) + p, own_ref).wait()
    factor = scale * math.log2(math.e)

    def keys_of(t):
        return keys_ref[pl.ds(pl.multiple_of(t * tile, tile), tile), :]

    def lane_parts(values):
        return [values[:, i * lanes : (i + 1) * lanes] for i in range(tile // lanes)]

    def score(t, masked):
        scores = lax.dot_general(
            full_ref[...], keys_of(t), (((1,), (1,)), ((), ())), preferred_element_type=jnp.float32
        )
        if masked:
            key = lax.broadcasted_iota(jnp.int32, scores.shape, 1) + t * tile
            query = lax.broadcasted_iota(jnp.int32, scores.shape, 0) + place * block_len
            scores = jnp.where(key <= query, scores, -1e30)
        scores_ref[t] = scores
        lane_ref[...] = functools.reduce(jnp.maximum, lane_parts(scores), lane_ref[...])

    lane_ref[...] = jnp.full(lane_ref.shape, -1e30, jnp.float32)

    @pl.loop(0, last)
    def _(t):
        wait_for(t)
        score(t, False)

    wait_for(last)
    score(last, True)
    highest = jnp.max(lane_ref[...], axis=1, keepdims=True) * factor
    lane_ref[...] = jnp.zeros(lane_ref.shape, jnp.float32)
    weight_ref[...] = jnp.zeros(weight_ref.shape, jnp.float32)

    @pl.loop(0, last + 1)
    def _(t):
        probs = jnp.exp2(scores_ref[t] * factor - highest)
        lane_ref[...] = functools.reduce(jnp.add, lane_parts(probs), lane_ref[...])
        weight_ref[...] += jnp.dot(
            probs.astype(jnp.bfloat16),
            keys_of(t)[:, :LATENT_WIDTH],
            preferred_element_type=jnp.float32,
        )

    weight_sum = jnp.sum(lane_ref[...], axis=1, keepdims=True)
    latent_out = (weight_ref[...] / weight_sum).astype(jnp.bfloat16)
    out_ref[...] = jnp.dot(
        latent_out, value_up_ref[...], preferred_element_type=jnp.float32
    ).astype(out_ref.dtype)

    @pl.loop(last + 1, scores_ref.shape[0])
    def _(t):
        wait_for(t)


def attend(queries, own, other, key_up, value_up, info, blocks, first, count):
    block_len = 2 * own.shape[0] // blocks
    head_width = queries.shape[1]
    tile = 2 * block_len
    hbm = pl.BlockSpec(memory_space=pl.ANY)
    return pl.pallas_call(
        functools.partial(
            attention_kernel, 1.0 / math.sqrt(PLAIN_HEAD_WIDTH + ROTARY_WIDTH), first
        ),
        grid_spec=pltpu.PrefetchScalarGridSpec(
            num_scalar_prefetch=1,
            grid=(count,),
            in_specs=[
                pl.BlockSpec((block_len, head_width), lambda i, info: (first + i, 0)),
                pl.BlockSpec(key_up.shape, lambda i, info: (0, 0)),
                pl.BlockSpec(value_up.shape, lambda i, info: (0, 0)),
                hbm,
                hbm,
            ],
            out_specs=pl.BlockSpec((block_len, VALUE_WIDTH), lambda i, info: (i, 0)),
            scratch_shapes=[
                pltpu.VMEM((blocks * block_len, own.shape[1]), jnp.bfloat16),
                pltpu.VMEM((block_len, own.shape[1]), jnp.bfloat16),
                pltpu.VMEM((blocks * block_len // tile, block_len, tile), jnp.float32),
                pltpu.VMEM((block_len, 128), jnp.float32),
                pltpu.VMEM((block_len, LATENT_WIDTH), jnp.float32),
                pltpu.SemaphoreType.DMA((blocks,)),
            ],
        ),
        out_shape=jax.ShapeDtypeStruct((count * block_len, VALUE_WIDTH), jnp.bfloat16),
        compiler_params=pltpu.CompilerParams(vmem_limit_bytes=VMEM_LIMIT),
        cost_estimate=LARGE,
        name="latent_attention",
    )(info, queries, key_up, value_up, own, other)


def shards(
    queries, latent, key_up_weight, value_up_weight, block_order, expert_ids, gates, expert_rows
):
    n_ctx, n_exp = lax.axis_size("ctx"), lax.axis_size("exp")
    devices = n_ctx * n_exp
    ctx = lax.axis_index("ctx").astype(jnp.int32)
    exp = lax.axis_index("exp").astype(jnp.int32)
    me = (ctx * n_exp + exp).reshape(1)
    capacity, model_width = expert_rows.shape[4:]
    rows = jnp.transpose(expert_rows[0, 0], (0, 2, 1, 3)).reshape(n_ctx, capacity * n_exp, model_width)
    count = n_exp // 4
    slots = jnp.arange(n_exp * capacity, dtype=jnp.int32)
    relative = slots // (count * capacity)
    low_bits = (exp & 3) ^ relative
    wanted = (slots % capacity) * n_exp + (slots // capacity) % count * 4 + low_bits
    select = (wanted[:, None] == slots[None, :]).astype(jnp.bfloat16)

    ctx1, side = ctx.reshape(1), ((exp >> 2) & 1).reshape(1)
    steps, tokens = len(STEPS), expert_ids.shape[0]
    packed, held, sent = [None] * steps, [[None] * 8 for _ in STEPS], []

    def pack_step(i, *others):
        start = sum(width for width, _ in STEPS[:i])
        return pack(after(ctx1, *others), select, rows, start, STEPS[i][0], i in LONG_PACKS)

    def send(i, parts, *others):
        for part in parts:
            mask = (part & 3) | (n_exp if part & 4 else 0)
            queue = sent[-IN_FLIGHT : 1 - IN_FLIGHT]
            held[i][part] = exchange(after(packed[i][part], *queue, *others), mask, devices)
            sent.append(held[i][part])

    packed[0] = pack_step(0)

    routes = jnp.concatenate([expert_ids.T.astype(jnp.float32), gates.T], axis=0)[None]
    routes = after(routes, packed[0][0])
    for bit in range(2, n_exp.bit_length() - 1):
        routes = jnp.concatenate([routes, exchange(routes, 1 << bit, devices)], axis=0)
    send(0, SENDS[:4])
    packed[1] = pack_step(1, packed[0][0])
    weights = combine_weights(after(me, packed[1][0]), routes, capacity, n_exp)
    send(0, SENDS[4:])
    send(1, SENDS[:4])
    last = [weights]

    latent = after(latent, packed[1][0])
    members = n_exp // 2
    share = latent.shape[0] // members
    place = (exp >> 2) * 2 + (exp & 1)
    mine = lax.dynamic_slice_in_dim(latent, place * share, share, axis=0)
    part = exchange(after(mine, *sent[:2]), n_exp, devices)
    groups = [[d for d in range(n_exp) if (d >> 1) & 1 == bit] for bit in range(2)]
    other = lax.all_gather(
        after(part, *sent[4:7]), "exp", axis=0, tiled=True, axis_index_groups=groups
    )

    blocks = block_order.shape[0]
    local_blocks = blocks // n_ctx
    ids = jnp.arange(blocks, dtype=jnp.int32)
    stored = jnp.sum(jnp.where(block_order[None, :] == ids[:, None], ids[None, :], 0), axis=1)
    query_block = lax.dynamic_slice_in_dim(block_order, ctx * local_blocks, local_blocks)
    info = jnp.concatenate([ctx1, stored // local_blocks, stored % local_blocks, query_block])
    heads = key_up_weight.shape[0]
    head_width = PLAIN_HEAD_WIDTH + ROTARY_WIDTH
    outputs, done_blocks = [], 0

    def attention_part(count, *last):
        nonlocal done_blocks
        part = []
        for h in range(heads):
            head_queries = queries[:, h * head_width : (h + 1) * head_width]
            part.append(
                attend(
                    head_queries,
                    latent,
                    other,
                    key_up_weight[h],
                    value_up_weight[h],
                    after(info, *last),
                    blocks,
                    done_blocks,
                    count,
                )
            )
        done_blocks += count
        outputs.append(part[0] if heads == 1 else jnp.concatenate(part, axis=1))
        return outputs[-1]

    def halve(total, bit):
        place = (exp >> bit) & 1
        pairs = total.reshape(-1, 2, tokens, total.shape[1])
        halves = (lax.dynamic_index_in_dim(pairs, p, 1, keepdims=False) for p in (place, 1 - place))
        return [half.reshape(-1, total.shape[1]) for half in halves]

    bits = range(2, n_exp.bit_length() - 1)
    halves = [None] * steps
    pieces = [None] * steps

    def begin(i, keep, send, bit, *others):
        halves[i] = (keep, exchange(after(send, *others), 1 << bit, devices), bit)

    def advance(i, *others):
        keep, got, bit = halves[i]
        keep = after(keep, *others)
        total = (keep.astype(jnp.float32) + got.astype(jnp.float32)).astype(jnp.bfloat16)
        if bit == bits[-1]:
            pieces[i] = total
        else:
            begin(i, *halve(total, bit + 1), bit + 1)

    axis_groups = [list(range(low, n_exp, 4)) for low in range(4)]
    for i, (_, scattered) in enumerate(STEPS):
        held[i][0] = packed[i][0]
        ready = [part] if i == 0 else []
        sums = partial_sums(weights, held[i], after(side, *last, *ready), tokens, not scattered)
        last = sums[:1]
        if i + 1 < steps:
            send(i + 1, SENDS[4:], *last)
        if QUERY_BLOCKS[i]:
            last = [attention_part(QUERY_BLOCKS[i], *last, pieces[i - 1])]
        for j in AHEAD[i]:
            packed[j] = pack_step(j, *last)
            last = packed[j][:1]
        if i + 2 < steps:
            send(i + 2, SENDS[:4])
        if not scattered:
            begin(i, *sums, bits[0])
        else:
            pieces[i] = lax.psum_scatter(
                after(sums[0], *[held[i + 1][part] for part in SENDS[: 0 if i else 4]]),
                "exp",
                scatter_dimension=0,
                axis_index_groups=axis_groups,
                tiled=True,
            )
    final = max(i for i, (_, scattered) in enumerate(STEPS) if scattered)
    pieces[final] = after(pieces[final], *last)
    while any(piece is None for piece in pieces):
        before = ()
        for i in range(steps):
            if pieces[i] is None:
                advance(i, *before)
                before = (halves[i][0] if pieces[i] is None else pieces[i],)
    combined = jnp.concatenate(pieces, axis=1)
    attended = jnp.concatenate(outputs, axis=0)
    return (attended, combined)


def solution(mesh):
    return jax.shard_map(
        shards,
        mesh=mesh,
        in_specs=(
            P("ctx", "exp"),
            P("ctx", None),
            P("exp", None, None),
            P("exp", None, None),
            P(),
            P(("ctx", "exp"), None),
            P(("ctx", "exp"), None),
            P("ctx", "exp", None, None, None, None),
        ),
        out_specs=(P("ctx", "exp"), P(("ctx", "exp"), None)),
        check_vma=False,
    )
```
